256 devices in a mesh: pts: 32 (over y, x, core), tm: 8 (over z).
Axes of the slice: x: 4, y: 4, z: 8, core: 2. Of those that a mesh axis runs over, the one named last changes fastest.
Arguments:
- record: float32 [128, 1536, 1024], P('tm', 'pts'), may hold values from -125 to 125
- start_time: float32 [128, 64], replicated, may hold values from -6 to 6
- start_circ: float32 [1024, 128], replicated, may hold values from -6 to 6
Outputs:
- factor_time: float32 [128, 64], replicated
- factor_circ: float32 [1024, 128], replicated
- core_tensor: float32 [64, 1536, 128], P('tm', 'pts')
The draws below stay inside these ranges and needn't reach their ends.
All inputs are finite; a program needn't handle non-finite values.
Results may differ from the reference program's by a relative error of at most 0.0003.
Values sent between devices are 32-bit elements; how exact they have to be, the bound alone decides.
A program may use at most 64 MiB of HBM per device.

```python
import jax
import jax.numpy as jnp
from jax import lax

NC = 1024
RT = 64
RC = 128
ITERS = 3
MF = 1536
NT = 128


def draw_record(key, part):
    key = jax.random.fold_in(key, 11)
    keys = jax.random.split(key, 11)
    noise = jnp.clip(jax.random.normal(keys[0], (NT, MF, NC), jnp.float32), -4.0, 4.0)
    time_scale = jnp.exp(jax.random.uniform(keys[1], (NT, 1, 1), jnp.float32, 0.0, 1.1))
    circ_scale = jnp.exp(jax.random.uniform(keys[2], (1, 1, NC), jnp.float32, 0.0, 1.1))
    wave_one = jnp.clip(jax.random.normal(keys[3], (NT, 1, 1), jnp.float32), -4.0, 4.0)
    wave_two = jnp.clip(jax.random.normal(keys[4], (NT, 1, 1), jnp.float32), -4.0, 4.0)
    shape_one = jnp.clip(jax.random.normal(keys[5], (1, MF, NC), jnp.float32), -4.0, 4.0)
    shape_two = jnp.clip(jax.random.normal(keys[6], (1, MF, NC), jnp.float32), -4.0, 4.0)
    lobe_one = jnp.clip(jax.random.normal(keys[7], (1, 1, NC), jnp.float32), -4.0, 4.0)
    lobe_two = jnp.clip(jax.random.normal(keys[8], (1, 1, NC), jnp.float32), -4.0, 4.0)
    field_one = jnp.clip(jax.random.normal(keys[9], (NT, MF, 1), jnp.float32), -4.0, 4.0)
    field_two = jnp.clip(jax.random.normal(keys[10], (NT, MF, 1), jnp.float32), -4.0, 4.0)
    shared = 0.15 * (wave_one * shape_one + wave_two * shape_two)
    shared = shared + 0.15 * (lobe_one * field_one + lobe_two * field_two)
    return time_scale * circ_scale * (noise + shared)


def scatter_about(key, shape, width, bound, kind=jnp.bfloat16):
    array = jax.random.normal(key, shape, jnp.float32) * width
    return jnp.minimum(jnp.maximum(array, -bound), bound).astype(kind)


def setup_inputs(seed: int = 0) -> dict:
    splits = jax.random.split(jax.random.key(seed), 4)
    record = draw_record(jax.random.fold_in(splits[3], 71), 0)
    start_time = scatter_about(splits[1], (NT, RT), 1.0, 6.0, jnp.float32)
    start_circ = scatter_about(splits[2], (NC, RC), 1.0, 6.0, jnp.float32)
    return {"record": record, "start_time": start_time, "start_circ": start_circ}


def orthonormal_iteration(gram_full, start):
    basis_now = start
    for repeat in range(ITERS):
        grown_full = jnp.dot(gram_full, basis_now, precision=lax.Precision.HIGHEST)
        inner_sum = jnp.dot(grown_full.T, grown_full, precision=lax.Precision.HIGHEST)
        factor_low = jnp.linalg.cholesky(inner_sum)
        basis_now = jax.scipy.linalg.solve_triangular(factor_low, grown_full.T, lower=True).T
    return basis_now

def reference(record, start_time, start_circ):
    gram_time = jnp.einsum('tpc,spc->ts', record, record, precision=lax.Precision.HIGHEST)
    factor_time = orthonormal_iteration(gram_time, start_time)
    reduced = jnp.einsum('tr,tpc->rpc', factor_time, record, precision=lax.Precision.HIGHEST)
    gram_circ = jnp.einsum('rpc,rpd->cd', reduced, reduced, precision=lax.Precision.HIGHEST)
    factor_circ = orthonormal_iteration(gram_circ, start_circ)
    core_tensor = jnp.einsum('rpc,ck->rpk', reduced, factor_circ, precision=lax.Precision.HIGHEST)
    return (factor_time, factor_circ, core_tensor)
```

```python
import functools

import jax
import jax.numpy as jnp
from jax import lax
from jax.experimental import pallas as pl
from jax.experimental.pallas import tpu as pltpu
from jax.sharding import PartitionSpec as P

ITERS = 3
MESH = pl.DeviceIdType.MESH
HI = lax.Precision.HIGHEST
F32 = jnp.float32
VM = pltpu.VMEM
LIMIT = 56 * 1024 * 1024
CHUNKS = 2
BLOCKS = 36


def dot(a, b, dims=((1,), (0,))):
    return lax.dot_general(a, b, (dims, ((), ())), precision=HI, preferred_element_type=F32)


def place():
    pts = lax.axis_index("pts")
    return pts // 8, (pts // 2) % 4, pts % 2, lax.axis_index("tm")


def device(y, x, c, z):
    return (y * 8 + x * 2 + c, z)


def greet(peers):
    barrier = pltpu.get_barrier_semaphore()
    for peer in peers:
        pl.semaphore_signal(barrier, inc=1, device_id=peer, device_id_type=MESH)
    pl.semaphore_wait(barrier, len(peers))


def send(src, dst, ssem, rsem, peer):
    copy = pltpu.make_async_remote_copy(
        src_ref=src, dst_ref=dst, send_sem=ssem, recv_sem=rsem, device_id=peer, device_id_type=MESH
    )
    copy.start()
    return copy


def exchange_kernel(rec, ex, gram, stage, part, col, plane, xs, xr, gs, gr):
    y, x, c, z = place()
    m = z * 2 + c
    q = y * 4 + x

    def column(d):
        other = (m + d) % 16
        return other, device(y, x, other % 2, other // 2)

    def flat(d):
        other = (q + d) % 16
        return device(other // 4, other % 4, c, z)

    greet([column(d)[1] for d in range(1, 16)] + [flat(d) for d in range(1, 16)])
    for zz in range(8):
        for p in range(6):
            for h in range(2):
                point = 6 * zz + p
                for b in range(8):
                    first = h * 8 * 384 + point // 8 * 64 + b * 8 + point % 8
                    stage[zz, p, pl.ds(8 * h, 8), 128 * b : 128 * (b + 1)] = rec[pl.ds(first, 8, stride=384), :]
    width = 6 // CHUNKS
    copies = []
    for k in range(CHUNKS):
        some = pl.ds(k * width, width)
        for d in (4, 3, 5, 2, 6, 1, 7):
            to = (z + d) % 8
            copies.append(
                (k, send(stage.at[to, some], ex.at[z, some], xs.at[k, d], xr.at[k, d], device(y, x, c, to)))
            )
    ex[z] = stage[z]
    total = jnp.zeros((128, 128), F32)
    for k in range(CHUNKS):
        for kk, copy in copies:
            if kk == k:
                copy.wait_recv()
        for p in range(k * width, (k + 1) * width):
            slab = ex[:, p].reshape(128, 1024)
            total = total + dot(slab, slab, ((1,), (1,)))
    for _, copy in copies:
        copy.wait_send()
    part[...] = total.reshape(16, 8, 128)
    copies = []
    for d in range(1, 16):
        other, peer = column(d)
        copies.append(send(part.at[other], col.at[m], gs.at[0, d], gr.at[0, d], peer))
    col[m] = part[m]
    for copy in copies:
        copy.wait()
    plane[q] = jnp.sum(col[...], axis=0)
    copies = []
    for d in range(1, 16):
        copies.append(send(plane.at[q], plane.at[q], gs.at[1, d], gr.at[1, d], flat(d)))
    for copy in copies:
        copy.wait()
    gram[m] = jnp.sum(plane[...], axis=0)
    copies = []
    for d in range(1, 16):
        copies.append(send(gram.at[m], gram.at[m], gs.at[2, d], gr.at[2, d], column(d)[1]))
    for copy in copies:
        copy.wait()


def exchange(record):
    return pl.pallas_call(
        exchange_kernel,
        out_shape=(jax.ShapeDtypeStruct((8, 6, 16, 1024), F32), jax.ShapeDtypeStruct((16, 8, 128), F32)),
        in_specs=[pl.BlockSpec(memory_space=VM)],
        out_specs=(pl.BlockSpec(memory_space=VM), pl.BlockSpec(memory_space=VM)),
        scratch_shapes=[
            VM((8, 6, 16, 1024), F32),
            VM((16, 8, 128), F32),
            VM((16, 8, 128), F32),
            VM((16, 8, 128), F32),
            pltpu.SemaphoreType.DMA((CHUNKS, 8)),
            pltpu.SemaphoreType.DMA((CHUNKS, 8)),
            pltpu.SemaphoreType.DMA((3, 16)),
            pltpu.SemaphoreType.DMA((3, 16)),
        ],
        compiler_params=pltpu.CompilerParams(collective_id=0, has_side_effects=True, vmem_limit_bytes=LIMIT),
        name="exchange",
    )(record)


def lower_inverse(w):
    n = w.shape[0]
    rows = lax.broadcasted_iota(jnp.int32, (8, 1), 0)
    eye = (lax.broadcasted_iota(jnp.int32, (n, n), 0) == lax.broadcasted_iota(jnp.int32, (n, n), 1)).astype(F32)
    both = jnp.concatenate([w, eye], axis=1)
    tiles = [both[8 * i : 8 * i + 8] for i in range(n // 8)]
    diag = []
    for j in range(n):
        own, inside = j // 8, j % 8
        row = tiles[own][inside : inside + 1]
        pivot = row[:, j : j + 1]
        diag.append(pivot)
        scaled = row * (1.0 / pivot)
        for i in range(own, n // 8):
            column = tiles[i][:, j : j + 1]
            if i == own:
                column = jnp.where(rows > inside, column, 0.0)
            tiles[i] = tiles[i] - column * scaled
    out = []
    for i in range(n // 8):
        d = jnp.concatenate(diag[8 * i : 8 * i + 8], axis=0)
        out.append(tiles[i][:, n:] * lax.rsqrt(d))
    return jnp.concatenate(out, axis=0)


def time_kernel(ex, gram, start, factor, reduced, circ, turned):
    g = gram[...].reshape(128, 128)
    factor[...] = start[...]

    def step(i, carry):
        grown = dot(g, factor[...])
        inner = dot(grown, grown, ((0,), (0,)))
        factor[...] = dot(grown, lower_inverse(inner), ((1,), (1,)))
        return carry

    lax.fori_loop(0, ITERS, step, 0)
    across = factor[...].T
    for p in range(6):
        reduced[pl.ds(64 * p, 64), :] = dot(across, ex[:, p].reshape(128, 1024))
    turned[...] = reduced[...].T
    for i in range(8):
        wide = dot(turned[pl.ds(128 * i, 128), :], reduced[:, : 128 * (i + 1)])
        for j in range(i + 1):
            circ[i * (i + 1) // 2 + j] = wide[:, 128 * j : 128 * (j + 1)]


def time_part(ex, gram, start):
    return pl.pallas_call(
        time_kernel,
        out_shape=(
            jax.ShapeDtypeStruct((128, 64), F32),
            jax.ShapeDtypeStruct((384, 1024), F32),
            jax.ShapeDtypeStruct((BLOCKS, 128, 128), F32),
        ),
        in_specs=[pl.BlockSpec(memory_space=VM)] * 3,
        out_specs=(pl.BlockSpec(memory_space=VM),) * 3,
        scratch_shapes=[VM((1024, 384), F32)],
        compiler_params=pltpu.CompilerParams(vmem_limit_bytes=LIMIT),
        name="time_part",
    )(ex, gram, start)


Y, X, C, Z = (0, 4), (1, 4), (2, 2), (3, 8)
PARTS = (
    (0, 256, (C, X, Y, Z)),
    (256, 256, (C, Y, X, Z)),
    (512, 64, (C, Z, X, Y)),
)


def sum_kernel(part, out, *scratch):
    here = place()

    def peer(axis, d):
        at = list(here)
        at[axis[0]] = (here[axis[0]] + d) % axis[1]
        return at[axis[0]], device(*at)

    greet([peer(axis, d)[1] for axis in (Y, X, C, Z) for d in range(1, axis[1])])
    places = [base for base, _, _ in PARTS]
    sizes = [size for _, size, _ in PARTS]
    bufs = [scratch[4 * n : 4 * n + 4] for n in range(3)]
    accs = scratch[12:15]
    ss, rs = scratch[15], scratch[16]
    trail = [[], [], []]
    for step in range(4):
        going = []
        for n, (_, _, order) in enumerate(PARTS):
            axis = order[step]
            me = here[axis[0]]
            split = sizes[n] % axis[1] == 0
            piece = sizes[n] // axis[1] if split else sizes[n]
            buf = bufs[n][step]
            src = part if step == 0 else accs[n]
            origin = places[n] if step == 0 else 0
            copies = []
            for d in range(1, axis[1]):
                other, dev = peer(axis, d)
                at = origin + other * piece if split else origin
                copies.append(
                    send(src.at[pl.ds(at, piece)], buf.at[me], ss.at[n, step, d], rs.at[n, step, d], dev)
                )
            mine = origin + me * piece if split else origin
            buf[me] = src[pl.ds(mine, piece)]
            going.append((n, axis, me, split, piece, buf, copies))
        for n, axis, me, split, piece, buf, copies in going:
            for copy in copies:
                copy.wait()
            value = buf[0]
            for k in range(1, axis[1]):
                value = value + buf[k]
            trail[n].append((axis, places[n], sizes[n], split))
            if split:
                places[n] = places[n] + me * piece
                sizes[n] = piece
            if step < 3:
                accs[n][pl.ds(0, piece)] = value
            else:
                out[pl.ds(places[n], piece)] = value
    for step in (3, 2, 1, 0):
        going = []
        for n in range(3):
            axis, was, size, split = trail[n][step]
            if split:
                some = out.at[pl.ds(places[n], sizes[n])]
                for d in range(1, axis[1]):
                    going.append(send(some, some, ss.at[n, 4 + step, d], rs.at[n, 4 + step, d], peer(axis, d)[1]))
                places[n], sizes[n] = was, size
        for copy in going:
            copy.wait()


def sum_parts(part):
    bufs, accs = [], []
    for _, size, order in PARTS:
        for step, axis in enumerate(order):
            if size % axis[1] == 0:
                size = size // axis[1]
            bufs.append(VM((axis[1], size, 8, 128), F32))
            if step == 0:
                accs.append(VM((size, 8, 128), F32))
    return pl.pallas_call(
        sum_kernel,
        out_shape=jax.ShapeDtypeStruct((BLOCKS * 16, 8, 128), F32),
        in_specs=[pl.BlockSpec(memory_space=VM)],
        out_specs=pl.BlockSpec(memory_space=VM),
        scratch_shapes=[
            *bufs,
            *accs,
            pltpu.SemaphoreType.DMA((3, 8, 8)),
            pltpu.SemaphoreType.DMA((3, 8, 8)),
        ],
        compiler_params=pltpu.CompilerParams(collective_id=1, has_side_effects=True, vmem_limit_bytes=LIMIT),
        name="sum_parts",
    )(part)


def circ_kernel(tri, start, reduced, factor, core, full):
    for i in range(8):
        for j in range(i + 1):
            block = tri[i * (i + 1) // 2 + j]
            full[pl.ds(128 * i, 128), 128 * j : 128 * (j + 1)] = block
            if j < i:
                full[pl.ds(128 * j, 128), 128 * i : 128 * (i + 1)] = block.T
    factor[...] = start[...]

    def step(i, carry):
        grown = dot(full[...], factor[...])
        inner = dot(grown, grown, ((0,), (0,)))
        factor[...] = dot(grown, lower_inverse(inner), ((1,), (1,)))
        return carry

    lax.fori_loop(0, ITERS, step, 0)
    for p in range(6):
        here = dot(reduced[pl.ds(64 * p, 64), :], factor[...])
        for k in range(8):
            core[k, p] = here[8 * k : 8 * k + 8]


def circ_part(tri, start, reduced):
    return pl.pallas_call(
        circ_kernel,
        out_shape=(jax.ShapeDtypeStruct((1024, 128), F32), jax.ShapeDtypeStruct((8, 6, 8, 128), F32)),
        in_specs=[pl.BlockSpec(memory_space=VM)] * 3,
        out_specs=(pl.BlockSpec(memory_space=VM),) * 2,
        scratch_shapes=[VM((1024, 1024), F32)],
        compiler_params=pltpu.CompilerParams(vmem_limit_bytes=LIMIT),
        name="circ_part",
    )(tri, start, reduced)


def return_kernel(core, out, got, ss, rs):
    y, x, c, z = place()
    greet([device(y, x, c, (z + d) % 8) for d in range(1, 8)])
    copies = []
    for d in (4, 3, 5, 2, 6, 1, 7):
        to = (z + d) % 8
        copies.append(send(core.at[to], got.at[z], ss.at[d], rs.at[d], device(y, x, c, to)))
    got[z] = core[z]
    for copy in copies:
        copy.wait()
    for k in range(8):
        for p in range(6):
            out[pl.ds(6 * k + p, 8, stride=48), :] = got[k, p]


def return_core(core):
    return pl.pallas_call(
        return_kernel,
        out_shape=jax.ShapeDtypeStruct((384, 128), F32),
        in_specs=[pl.BlockSpec(memory_space=VM)],
        out_specs=pl.BlockSpec(memory_space=VM),
        scratch_shapes=[
            VM((8, 6, 8, 128), F32),
            pltpu.SemaphoreType.DMA((8,)),
            pltpu.SemaphoreType.DMA((8,)),
        ],
        compiler_params=pltpu.CompilerParams(collective_id=2, has_side_effects=True, vmem_limit_bytes=LIMIT),
        name="return_core",
    )(core)


def local(record, start_time, start_circ):
    rows = record.reshape(96, 8, 8, 128).transpose(0, 2, 1, 3).reshape(6144, 128)
    ex, gram = exchange(rows)
    factor_time, reduced, part = time_part(ex, gram, start_time)
    tri = sum_parts(part.reshape(BLOCKS * 16, 8, 128))
    factor_circ, core = circ_part(tri.reshape(BLOCKS, 128, 128), start_circ, reduced)
    core = return_core(core).reshape(8, 48, 128)
    return (factor_time, factor_circ, core)


def solution(mesh):
    placed = (P("tm", "pts", None), P(), P())
    return jax.shard_map(
        local,
        mesh=mesh,
        in_specs=placed,
        out_specs=(P(), P(), P("tm", "pts", None)),
        check_vma=False,
    )
```

```python
import functools

import jax
import jax.numpy as jnp
from jax import lax
from jax.experimental import pallas as pl
from jax.experimental.pallas import tpu as pltpu
from jax.sharding import PartitionSpec as P

ITERS = 3
MESH = pl.DeviceIdType.MESH
HI = lax.Precision.HIGHEST
F32 = jnp.float32
BF16 = jnp.bfloat16
VM = pltpu.VMEM
LIMIT = 56 * 1024 * 1024
CHUNKS = 6
WIDTH = 6 // CHUNKS
TERMS = ((0, 0), (0, 1), (1, 0), (0, 2), (1, 1), (2, 0))
BLOCKS = 36


def dot(a, b, dims=((1,), (0,))):
    return lax.dot_general(a, b, (dims, ((), ())), precision=HI, preferred_element_type=F32)


def place():
    pts = lax.axis_index("pts")
    return pts // 8, (pts // 2) % 4, pts % 2, lax.axis_index("tm")


def device(y, x, c, z):
    return (y * 8 + x * 2 + c, z)


def send(src, dst, ssem, rsem, peer):
    copy = pltpu.make_async_remote_copy(
        src_ref=src, dst_ref=dst, send_sem=ssem, recv_sem=rsem, device_id=peer, device_id_type=MESH
    )
    copy.start()
    return copy


def lower_inverse(w):
    n = w.shape[0]
    count = n // 8
    lane = lax.broadcasted_iota(jnp.int32, (8, 128), 1)
    sub = lax.broadcasted_iota(jnp.int32, (8, 128), 0)

    def unit(i):
        return (lane == sub + 8 * i + 128 - n).astype(F32)

    if n == 128:
        parts = [[w[8 * i : 8 * i + 8] for i in range(count)], [unit(i) for i in range(count)]]
    else:
        both = jnp.concatenate([w, jnp.zeros_like(w)], axis=1)
        parts = [[both[8 * i : 8 * i + 8] + unit(i) for i in range(count)]]

    def over_lanes(v, j):
        return jnp.broadcast_to(v[:, j : j + 1], (8, 128))

    def over_rows(v, m):
        return jnp.broadcast_to(v[m : m + 1, :], (8, 128))

    out = []
    for k in range(count):
        columns = [[over_lanes(parts[0][i], 8 * k + l) for l in range(8)] for i in range(k, count)]
        e = [[over_rows(columns[0][l], m) for l in range(m + 1)] for m in range(8)]
        t = [[None] * 8 for _ in range(8)]
        inverse = []
        for l in range(8):
            inverse.append(1.0 / e[l][l])
            for m in range(l + 1, 8):
                f = e[m][l] * inverse[l]
                for j in range(l + 1, m + 1):
                    e[m][j] = e[m][j] - f * e[j][l]
                for j in range(l):
                    t[m][j] = t[m][j] - f * t[l][j]
                t[m][l] = -f
        for part in parts:
            rows = [over_rows(part[k], m) for m in range(8)]
            done = []
            for m in range(8):
                v = rows[m]
                for j in range(m):
                    v = v + t[m][j] * rows[j]
                done.append(v)
            if k < count - 1:
                scaled = [done[m] * inverse[m] for m in range(8)]
                taken = []
                for l in range(8):
                    v = scaled[l]
                    for m in range(l + 1, 8):
                        v = v + t[m][l] * scaled[m]
                    taken.append(v)
                for i in range(k + 1, count):
                    v = part[i]
                    for l in range(8):
                        v = v - columns[i - k][l] * taken[l]
                    part[i] = v
        tile = done[0] * lax.rsqrt(e[0][0])
        for m in range(1, 8):
            tile = jnp.where(sub == m, done[m] * lax.rsqrt(e[m][m]), tile)
        out.append(tile[:, 128 - n :])
    return jnp.concatenate(out, axis=0)


def split(v):
    high = v.astype(BF16)
    rest = v - high.astype(F32)
    middle = rest.astype(BF16)
    return high, middle, (rest - middle.astype(F32)).astype(BF16)


def narrow(a, b):
    return lax.dot_general(a, b, (((1,), (0,)), ((), ())), preferred_element_type=F32)


def iterate(basis, grow):
    def step(i, carry):
        grown = grow(basis[...])
        inner = dot(grown, grown, ((1,), (1,)))
        basis[...] = dot(lower_inverse(inner), grown)
        return carry

    lax.fori_loop(0, ITERS, step, 0)


Y, X, C, Z = (0, 4), (1, 4), (2, 2), (3, 8)
PARTS = (
    (0, 256, (C, X, Y, Z)),
    (256, 256, (C, Y, X, Z)),
    (512, 64, (C, Z, X, Y)),
)


def first_kernel(
    rec, start, start_circ, basis, factor, mine, stage, ex, part, col, plane, gram, reduced, left, right, circ, tri, *scratch
):
    one, two, three, xs, xr, gs, gr, ms, mr, ss, rs, *scratch = scratch
    here = place()
    y, x, c, z = here
    m = z * 2 + c
    q = y * 4 + x

    def column(d):
        other = (m + d) % 16
        return other, device(y, x, other % 2, other // 2)

    def flat(d):
        other = (q + d) % 16
        return device(other // 4, other % 4, c, z)

    barrier = pltpu.get_barrier_semaphore()
    for d in range(1, 16):
        pl.semaphore_signal(barrier, inc=1, device_id=column(d)[1], device_id_type=MESH)
        pl.semaphore_signal(barrier, inc=1, device_id=flat(d), device_id_type=MESH)

    for k in range(CHUNKS):
        for zz in range(8):
            for p in range(k * WIDTH, (k + 1) * WIDTH):
                point = 6 * zz + p
                for h in range(2):
                    for b in range(8):
                        at = h * 8 * 384 + point // 8 * 64 + b * 8 + point % 8
                        stage[zz, p, pl.ds(8 * h, 8), 128 * b : 128 * (b + 1)] = rec[pl.ds(at, 8, stride=384), :]
    pl.semaphore_wait(barrier, 30)
    copies = []
    for k in range(CHUNKS):
        some = pl.ds(k * WIDTH, WIDTH)
        for d in (4, 3, 5, 2, 6, 1, 7):
            to = (z + d) % 8
            copies.append(
                (k, send(stage.at[to, some], ex.at[z, some], xs.at[k, d], xr.at[k, d], device(y, x, c, to)))
            )
    ex[z] = stage[z]
    total = jnp.zeros((128, 128), F32)
    for k in range(CHUNKS):
        for kk, copy in copies:
            if kk == k:
                copy.wait_recv()
        for p in range(k * WIDTH, (k + 1) * WIDTH):
            slab = ex[:, p].reshape(128, 1024)
            total = total + dot(slab, slab, ((1,), (1,)))
    started = [copy for _, copy in copies]

    part[...] = total.reshape(16, 8, 128)
    copies = []
    for d in range(1, 16):
        other, peer = column(d)
        copies.append(send(part.at[other], col.at[m], gs.at[0, d], gr.at[0, d], peer))
    col[m] = part[m]
    started += copies
    for copy in copies:
        copy.wait_recv()
    plane[q] = jnp.sum(col[...], axis=0)
    copies = []
    for d in range(1, 16):
        copies.append(send(plane.at[q], plane.at[q], gs.at[1, d], gr.at[1, d], flat(d)))
    started += copies
    for copy in copies:
        copy.wait_recv()
    gram[m] = jnp.sum(plane[...], axis=0)
    copies = []
    for d in range(1, 16):
        copies.append(send(gram.at[m], gram.at[m], gs.at[2, d], gr.at[2, d], column(d)[1]))
    started += copies
    for copy in copies:
        copy.wait_recv()
    for copy in started:
        copy.wait_send()

    g = gram[...].reshape(128, 128)
    factor[...] = start[...]
    iterate(factor, lambda basis: dot(basis, g))
    high, middle, lower = split(factor[...])
    most = jnp.concatenate([high, middle], axis=0)
    whole = jnp.concatenate([high, middle, lower], axis=0)
    for p in range(6):
        first, second, third = split(ex[:, p].reshape(128, 1024))
        u = narrow(whole, first)
        v = narrow(most, second)
        w = narrow(high, third)
        value = u[:64] + ((u[64:128] + v[:64]) + (u[128:] + v[64:] + w))
        reduced[p] = value.reshape(8, 8, 1024)
        pieces = split(value)
        turned = split(value.T)
        for k, (i, j) in enumerate(TERMS):
            left[:, 384 * k + 64 * p : 384 * k + 64 * (p + 1)] = turned[i]
            right[pl.ds(384 * k + 64 * p, 64), :] = pieces[j]
    mine[z] = reduced[:, z]
    returned = []

    def background():
        for d in (4, 3, 5, 2, 6, 1, 7):
            to = (z + d) % 8
            returned.append(send(reduced.at[:, to], mine.at[z], ms.at[d], mr.at[d], device(y, x, c, to)))

    for j in range(4):
        wide = narrow(left[pl.ds(256 * j, 1024 - 256 * j), :], right[:, 256 * j : 256 * (j + 1)])
        for b in (2 * j, 2 * j + 1):
            for a in range(b, 8):
                block = wide[128 * (a - 2 * j) : 128 * (a - 2 * j + 1), 128 * (b - 2 * j) : 128 * (b - 2 * j + 1)]
                circ[pl.ds((a * (a + 1) // 2 + b) * 16, 16)] = block.reshape(16, 8, 128)
    sum_over_devices(here, circ, tri, ss, rs, scratch, background)

    for i in range(8):
        for j in range(i + 1):
            block = tri[pl.ds((i * (i + 1) // 2 + j) * 16, 16)].reshape(128, 128)
            for full, piece in zip((one, two, three), split(block)):
                full[pl.ds(128 * i, 128), 128 * j : 128 * (j + 1)] = piece
            if j < i:
                for full, piece in zip((one, two, three), split(block.T)):
                    full[pl.ds(128 * j, 128), 128 * i : 128 * (i + 1)] = piece
    basis[...] = start_circ[...].T

    def grow(now):
        high, middle, low = split(now)
        a = narrow(jnp.concatenate([high, middle, low], axis=0), one[...])
        b = narrow(jnp.concatenate([high, middle], axis=0), two[...])
        c = narrow(high, three[...])
        return a[:128] + ((a[128:256] + b[:128]) + (a[256:] + b[128:] + c))

    iterate(basis, grow)
    for copy in returned:
        copy.wait()


def sum_over_devices(here, part, out, ss, rs, scratch, background):
    def peer(axis, d):
        at = list(here)
        at[axis[0]] = (here[axis[0]] + d) % axis[1]
        return at[axis[0]], device(*at)

    number = len(PARTS)
    bufs = [scratch[4 * n : 4 * n + 4] for n in range(number)]
    accs = scratch[4 * number : 5 * number]
    started = []
    going = [None] * number
    trail = [[] for _ in PARTS]
    places = [base for base, _, _ in PARTS]
    sizes = [size for _, size, _ in PARTS]

    for n, (base, size, order) in enumerate(PARTS):
        axis, nearby = order[:2]
        piece = size // 2 // nearby[1]
        other, dev = peer(axis, 1)
        going[n] = {}
        for d in (2, 1, 3, 0) if nearby[1] == 4 else (4, 3, 5, 2, 6, 1, 7, 0):
            to = peer(nearby, d)[0]
            some = part.at[pl.ds(base + other * (size // 2) + to * piece, piece)]
            going[n][d] = send(some, bufs[n][0].at[pl.ds(to * piece, piece)], ss.at[n, 0, d], rs.at[n, 0, d], dev)
        started += going[n].values()
    for n, (base, size, order) in enumerate(PARTS):
        axis, nearby = order[:2]
        trail[n].append((axis, base, size, False))
        sizes[n] = size // 2
        places[n] = base + here[axis[0]] * sizes[n]
        trail[n].append((nearby, places[n], sizes[n], False))
        piece = sizes[n] // nearby[1]
        copies = []
        for d, copy in going[n].items():
            copy.wait_recv()
            to, dev = peer(nearby, d)
            some = pl.ds(to * piece, piece)
            accs[n][some] = part[pl.ds(places[n] + to * piece, piece)] + bufs[n][0][some]
            if d:
                copies.append(send(accs[n].at[some], bufs[n][1].at[d], ss.at[n, 1, d], rs.at[n, 1, d], dev))
        going[n] = copies

    def scatter(n, step):
        axis = PARTS[n][2][step]
        me = here[axis[0]]
        buf = bufs[n][step]
        whole = sizes[n] % axis[1] != 0
        piece = sizes[n] if whole else sizes[n] // axis[1]
        copies = []
        for d in range(1, axis[1]):
            other, dev = peer(axis, d)
            some = accs[n].at[pl.ds(0 if whole else other * piece, piece)]
            copies.append(send(some, buf.at[me if whole else d], ss.at[n, step, d], rs.at[n, step, d], dev))
        if whole:
            buf[me] = accs[n][pl.ds(0, piece)]
        going[n] = copies
        trail[n].append((axis, places[n], sizes[n], whole))

    def add(n, step):
        axis, was, size, whole = trail[n][step]
        me = here[axis[0]]
        buf = bufs[n][step]
        for copy in going[n]:
            copy.wait()
        if whole:
            piece = size
            value = buf[0]
        else:
            piece = size // axis[1]
            value = accs[n][pl.ds(me * piece, piece)]
            places[n] = was + me * piece
            sizes[n] = piece
        for k in range(1, axis[1]):
            value = value + buf[k]
        if step == 3:
            out[pl.ds(places[n], piece)] = value
        else:
            accs[n][pl.ds(0, piece)] = value

    def gather(n, step):
        axis, was, size, whole = trail[n][step]
        copies = []
        if not whole:
            some = out.at[pl.ds(places[n], sizes[n])]
            for d in range(1, axis[1]):
                copies.append(send(some, some, ss.at[n, 4 + step, d], rs.at[n, 4 + step, d], peer(axis, d)[1]))
        going[n] = copies
        started.extend(copies)

    def forward(n, d):
        axis = PARTS[n][2][1]
        some = out.at[pl.ds(trail[n][1][1] + peer(axis, axis[1] - d)[0] * sizes[n], sizes[n])]
        return send(some, some, ss.at[n, 4, d], rs.at[n, 4, d], peer(C, 1)[1])

    for step in (1, 2, 3):
        for n in range(number):
            add(n, step)
            if step < 3:
                scatter(n, step + 1)
            else:
                gather(n, 3)
    for step in (2, 1):
        for n in range(number):
            for copy in going[n]:
                copy.wait_recv()
            if not trail[n][step + 1][3]:
                places[n], sizes[n] = trail[n][step + 1][1:3]
            gather(n, step)
            if step == 1:
                going[n] = list(enumerate(going[n], 1)), [forward(n, 0)]
    for n in range(number):
        coming, passed = going[n]
        for d, copy in coming:
            copy.wait_recv()
            passed.append(forward(n, d))
        started += passed
    background()
    for n in range(number):
        for copy in going[n][1]:
            copy.wait_recv()
    for copy in started:
        copy.wait_send()


def first_part(rows, start, start_circ):
    bufs, accs = [], []
    for _, size, order in PARTS:
        for step, axis in enumerate(order):
            if size % axis[1] == 0:
                size = size // axis[1]
            bufs.append(VM((axis[1], size, 8, 128) if step else (size, 8, 128), F32))
            if step == 0:
                accs.append(VM((size, 8, 128), F32))
    dma = pltpu.SemaphoreType.DMA
    return pl.pallas_call(
        first_kernel,
        out_shape=(
            jax.ShapeDtypeStruct((128, 1024), F32),
            jax.ShapeDtypeStruct((64, 128), F32),
            jax.ShapeDtypeStruct((8, 6, 8, 1024), F32),
        ),
        in_specs=[pl.BlockSpec(memory_space=VM)] * 3,
        out_specs=(pl.BlockSpec(memory_space=VM),) * 3,
        scratch_shapes=[
            VM((8, 6, 16, 1024), F32),
            VM((8, 6, 16, 1024), F32),
            VM((16, 8, 128), F32),
            VM((16, 8, 128), F32),
            VM((16, 8, 128), F32),
            VM((16, 8, 128), F32),
            VM((6, 8, 8, 1024), F32),
            VM((1024, 384 * len(TERMS)), BF16),
            VM((384 * len(TERMS), 1024), BF16),
            VM((BLOCKS * 16, 8, 128), F32),
            VM((BLOCKS * 16, 8, 128), F32),
            VM((1024, 1024), BF16),
            VM((1024, 1024), BF16),
            VM((1024, 1024), BF16),
            dma((CHUNKS, 8)),
            dma((CHUNKS, 8)),
            dma((3, 16)),
            dma((3, 16)),
            dma((8,)),
            dma((8,)),
            dma((len(PARTS), 8, 8)),
            dma((len(PARTS), 8, 8)),
            *bufs,
            *accs,
        ],
        compiler_params=pltpu.CompilerParams(collective_id=0, has_side_effects=True, vmem_limit_bytes=LIMIT),
        name="first_part",
    )(rows, start, start_circ)


def core_kernel(basis, mine, early, factor, core, late):
    late[...] = early[...]
    last = basis[...].T
    factor[...] = last
    here = dot(mine[...].reshape(384, 1024), last)
    for k in range(48):
        core[pl.ds(k, 8, stride=48), :] = here[8 * k : 8 * k + 8]


def core_part(basis, mine, early):
    return pl.pallas_call(
        core_kernel,
        out_shape=(
            jax.ShapeDtypeStruct((1024, 128), F32),
            jax.ShapeDtypeStruct((384, 128), F32),
            jax.ShapeDtypeStruct((64, 128), F32),
        ),
        in_specs=[pl.BlockSpec(memory_space=VM)] * 3,
        out_specs=(pl.BlockSpec(memory_space=VM),) * 3,
        compiler_params=pltpu.CompilerParams(vmem_limit_bytes=LIMIT),
        name="core_part",
    )(basis, mine, early)


def local(record, start_time, start_circ):
    rows = record.reshape(96, 8, 8, 128).transpose(0, 2, 1, 3).reshape(6144, 128)
    basis, early, mine = first_part(rows, start_time.T, start_circ)
    factor_circ, core, late = core_part(basis, mine, early)
    return (late.T, factor_circ, core.reshape(8, 48, 128))


def solution(mesh):
    placed = (P("tm", "pts", None), P(), P())
    return jax.shard_map(
        local,
        mesh=mesh,
        in_specs=placed,
        out_specs=(P(), P(), P("tm", "pts", None)),
        check_vma=False,
    )
```

```python
import functools

import jax
import jax.numpy as jnp
from jax import lax
from jax.experimental import pallas as pl
from jax.experimental.pallas import tpu as pltpu
from jax.sharding import PartitionSpec as P

ITERS = 3
MESH = pl.DeviceIdType.MESH
HI = lax.Precision.HIGHEST
F32 = jnp.float32
BF16 = jnp.bfloat16
VM = pltpu.VMEM
LIMIT = 56 * 1024 * 1024
CHUNKS = 6
WIDTH = 6 // CHUNKS
TERMS = ((0, 0), (0, 1), (1, 0))
BLOCKS = 36


def dot(a, b, dims=((1,), (0,))):
    return lax.dot_general(a, b, (dims, ((), ())), precision=HI, preferred_element_type=F32)


def place():
    pts = lax.axis_index("pts")
    return pts // 8, (pts // 2) % 4, pts % 2, lax.axis_index("tm")


def device(y, x, c, z):
    return (y * 8 + x * 2 + c, z)


def send(src, dst, ssem, rsem, peer):
    copy = pltpu.make_async_remote_copy(
        src_ref=src, dst_ref=dst, send_sem=ssem, recv_sem=rsem, device_id=peer, device_id_type=MESH
    )
    copy.start()
    return copy


def lower_inverse(w):
    n = w.shape[0]
    count = n // 8
    lane = lax.broadcasted_iota(jnp.int32, (8, 128), 1)
    sub = lax.broadcasted_iota(jnp.int32, (8, 128), 0)

    def unit(i):
        return (lane == sub + 8 * i + 128 - n).astype(F32)

    if n == 128:
        parts = [[w[8 * i : 8 * i + 8] for i in range(count)], [unit(i) for i in range(count)]]
    else:
        both = jnp.concatenate([w, jnp.zeros_like(w)], axis=1)
        parts = [[both[8 * i : 8 * i + 8] + unit(i) for i in range(count)]]

    def over_lanes(v, j):
        return jnp.broadcast_to(v[:, j : j + 1], (8, 128))

    def over_rows(v, m):
        return jnp.broadcast_to(v[m : m + 1, :], (8, 128))

    out = []
    for k in range(count):
        columns = [[over_lanes(parts[0][i], 8 * k + l) for l in range(8)] for i in range(k, count)]
        e = [[over_rows(columns[0][l], m) for l in range(m + 1)] for m in range(8)]
        t = [[None] * 8 for _ in range(8)]
        inverse = []
        for l in range(8):
            inverse.append(1.0 / e[l][l])
            for m in range(l + 1, 8):
                f = e[m][l] * inverse[l]
                for j in range(l + 1, m + 1):
                    e[m][j] = e[m][j] - f * e[j][l]
                for j in range(l):
                    t[m][j] = t[m][j] - f * t[l][j]
                t[m][l] = -f
        for part in parts:
            rows = [over_rows(part[k], m) for m in range(8)]
            done = []
            for m in range(8):
                v = rows[m]
                for j in range(m):
                    v = v + t[m][j] * rows[j]
                done.append(v)
            if k < count - 1:
                scaled = [done[m] * inverse[m] for m in range(8)]
                taken = []
                for l in range(8):
                    v = scaled[l]
                    for m in range(l + 1, 8):
                        v = v + t[m][l] * scaled[m]
                    taken.append(v)
                for i in range(k + 1, count):
                    v = part[i]
                    for l in range(8):
                        v = v - columns[i - k][l] * taken[l]
                    part[i] = v
        tile = done[0] * lax.rsqrt(e[0][0])
        for m in range(1, 8):
            tile = jnp.where(sub == m, done[m] * lax.rsqrt(e[m][m]), tile)
        out.append(tile[:, 128 - n :])
    return jnp.concatenate(out, axis=0)


def split(v):
    high = v.astype(BF16)
    rest = v - high.astype(F32)
    middle = rest.astype(BF16)
    return high, middle, (rest - middle.astype(F32)).astype(BF16)


def narrow(a, b):
    return lax.dot_general(a, b, (((1,), (0,)), ((), ())), preferred_element_type=F32)


def iterate(basis, grow):
    def step(i, carry):
        grown = grow(basis[...])
        inner = dot(grown, grown, ((1,), (1,)))
        basis[...] = dot(lower_inverse(inner), grown)
        return carry

    lax.fori_loop(0, ITERS, step, 0)


Y, X, C, Z = (0, 4), (1, 4), (2, 2), (3, 8)
PARTS = (
    (0, 256, (C, X, Y, Z)),
    (256, 256, (C, Y, X, Z)),
    (512, 64, (C, Z, X, Y)),
)


def first_kernel(
    rec, start, start_circ, basis, factor, mine, stage, ex, part, col, plane, gram, reduced, left, right, circ, tri, *scratch
):
    one, two, three, xs, xr, gs, gr, ms, mr, ss, rs, *scratch = scratch
    here = place()
    y, x, c, z = here
    m = z * 2 + c
    q = y * 4 + x

    def column(d):
        other = (m + d) % 16
        return other, device(y, x, other % 2, other // 2)

    def flat(d):
        other = (q + d) % 16
        return device(other // 4, other % 4, c, z)

    barrier = pltpu.get_barrier_semaphore()
    for d in range(1, 16):
        pl.semaphore_signal(barrier, inc=1, device_id=column(d)[1], device_id_type=MESH)
        pl.semaphore_signal(barrier, inc=1, device_id=flat(d), device_id_type=MESH)

    for k in range(CHUNKS):
        for zz in range(8):
            for p in range(k * WIDTH, (k + 1) * WIDTH):
                point = 6 * zz + p
                for h in range(2):
                    for b in range(8):
                        at = h * 8 * 384 + point // 8 * 64 + b * 8 + point % 8
                        stage[zz, p, pl.ds(8 * h, 8), 128 * b : 128 * (b + 1)] = rec[pl.ds(at, 8, stride=384), :]
    pl.semaphore_wait(barrier, 30)
    copies = []
    for k in range(CHUNKS):
        some = pl.ds(k * WIDTH, WIDTH)
        for d in (4, 3, 5, 2, 6, 1, 7):
            to = (z + d) % 8
            copies.append(
                (k, send(stage.at[to, some], ex.at[z, some], xs.at[k, d], xr.at[k, d], device(y, x, c, to)))
            )
    ex[z] = stage[z]
    total = jnp.zeros((128, 128), F32)
    for k in range(CHUNKS):
        for kk, copy in copies:
            if kk == k:
                copy.wait_recv()
        for p in range(k * WIDTH, (k + 1) * WIDTH):
            slab = ex[:, p].reshape(128, 1024)
            total = total + dot(slab, slab, ((1,), (1,)))
    started = [copy for _, copy in copies]

    part[...] = total.reshape(16, 8, 128)
    copies = []
    for d in range(1, 16):
        other, peer = column(d)
        copies.append(send(part.at[other], col.at[m], gs.at[0, d], gr.at[0, d], peer))
    col[m] = part[m]
    started += copies
    for copy in copies:
        copy.wait_recv()
    plane[q] = jnp.sum(col[...], axis=0)
    copies = []
    for d in range(1, 16):
        copies.append(send(plane.at[q], plane.at[q], gs.at[1, d], gr.at[1, d], flat(d)))
    started += copies
    for copy in copies:
        copy.wait_recv()
    gram[m] = jnp.sum(plane[...], axis=0)
    copies = []
    for d in range(1, 16):
        copies.append(send(gram.at[m], gram.at[m], gs.at[2, d], gr.at[2, d], column(d)[1]))
    started += copies
    for copy in copies:
        copy.wait_recv()
    for copy in started:
        copy.wait_send()

    g = gram[...].reshape(128, 128)
    factor[...] = start[...]
    iterate(factor, lambda basis: dot(basis, g))
    high, middle, lower = split(factor[...])
    most = jnp.concatenate([high, middle], axis=0)
    whole = jnp.concatenate([high, middle, lower], axis=0)
    returned = []

    def give_back(k, some):
        for d in (4, 3, 5, 2, 6, 1, 7):
            to = (z + d) % 8
            returned.append(
                send(reduced.at[some, to], mine.at[z, some], ms.at[k, d], mr.at[k, d], device(y, x, c, to))
            )

    for p in range(6):
        first, second, third = split(ex[:, p].reshape(128, 1024))
        u = narrow(whole, first)
        v = narrow(most, second)
        w = narrow(high, third)
        value = u[:64] + ((u[64:128] + v[:64]) + (u[128:] + v[64:] + w))
        reduced[p] = value.reshape(8, 8, 1024)
        if p == 0:
            give_back(0, pl.ds(0, 1))
        pieces = split(value)
        turned = split(value.T)
        for k, (i, j) in enumerate(TERMS):
            left[:, 384 * k + 64 * p : 384 * k + 64 * (p + 1)] = turned[i]
            right[pl.ds(384 * k + 64 * p, 64), :] = pieces[j]
    mine[z] = reduced[:, z]
    for j in range(4):
        wide = narrow(left[pl.ds(256 * j, 1024 - 256 * j), :], right[:, 256 * j : 256 * (j + 1)])
        for b in (2 * j, 2 * j + 1):
            for a in range(b, 8):
                block = wide[128 * (a - 2 * j) : 128 * (a - 2 * j + 1), 128 * (b - 2 * j) : 128 * (b - 2 * j + 1)]
                circ[pl.ds((a * (a + 1) // 2 + b) * 16, 16)] = block.reshape(16, 8, 128)
    sum_over_devices(here, circ, tri, ss, rs, scratch, lambda: give_back(1, pl.ds(1, 5)))

    for i in range(8):
        for j in range(i + 1):
            block = tri[pl.ds((i * (i + 1) // 2 + j) * 16, 16)].reshape(128, 128)
            for full, piece in zip((one, two, three), split(block)):
                full[pl.ds(128 * i, 128), 128 * j : 128 * (j + 1)] = piece
            if j < i:
                for full, piece in zip((one, two, three), split(block.T)):
                    full[pl.ds(128 * j, 128), 128 * i : 128 * (i + 1)] = piece
    basis[...] = start_circ[...].T

    def grow(now):
        high, middle, low = split(now)
        a = narrow(jnp.concatenate([high, middle, low], axis=0), one[...])
        b = narrow(jnp.concatenate([high, middle], axis=0), two[...])
        c = narrow(high, three[...])
        return a[:128] + ((a[128:256] + b[:128]) + (a[256:] + b[128:] + c))

    iterate(basis, grow)
    for copy in returned:
        copy.wait()


def sum_over_devices(here, part, out, ss, rs, scratch, background):
    def peer(axis, d):
        at = list(here)
        at[axis[0]] = (here[axis[0]] + d) % axis[1]
        return at[axis[0]], device(*at)

    number = len(PARTS)
    bufs = [scratch[4 * n : 4 * n + 4] for n in range(number)]
    accs = scratch[4 * number : 5 * number]
    started = []
    going = [None] * number
    trail = [[] for _ in PARTS]
    places = [base for base, _, _ in PARTS]
    sizes = [size for _, size, _ in PARTS]

    for n, (base, size, order) in enumerate(PARTS):
        axis, nearby = order[:2]
        piece = size // 2 // nearby[1]
        other, dev = peer(axis, 1)
        going[n] = {}
        for d in (2, 1, 3, 0) if nearby[1] == 4 else (4, 3, 5, 2, 6, 1, 7, 0):
            to = peer(nearby, d)[0]
            some = part.at[pl.ds(base + other * (size // 2) + to * piece, piece)]
            going[n][d] = send(some, bufs[n][0].at[pl.ds(to * piece, piece)], ss.at[n, 0, d], rs.at[n, 0, d], dev)
        started += going[n].values()
    for n, (base, size, order) in enumerate(PARTS):
        axis, nearby = order[:2]
        trail[n].append((axis, base, size, False))
        sizes[n] = size // 2
        places[n] = base + here[axis[0]] * sizes[n]
        trail[n].append((nearby, places[n], sizes[n], False))
        piece = sizes[n] // nearby[1]
        copies = []
        for d, copy in going[n].items():
            copy.wait_recv()
            to, dev = peer(nearby, d)
            some = pl.ds(to * piece, piece)
            accs[n][some] = part[pl.ds(places[n] + to * piece, piece)] + bufs[n][0][some]
            if d:
                copies.append(send(accs[n].at[some], bufs[n][1].at[d], ss.at[n, 1, d], rs.at[n, 1, d], dev))
        going[n] = copies

    def scatter(n, step):
        axis = PARTS[n][2][step]
        me = here[axis[0]]
        buf = bufs[n][step]
        whole = sizes[n] % axis[1] != 0
        piece = sizes[n] if whole else sizes[n] // axis[1]
        copies = []
        for d in range(1, axis[1]):
            other, dev = peer(axis, d)
            some = accs[n].at[pl.ds(0 if whole else other * piece, piece)]
            copies.append(send(some, buf.at[me if whole else d], ss.at[n, step, d], rs.at[n, step, d], dev))
        if whole:
            buf[me] = accs[n][pl.ds(0, piece)]
        going[n] = copies
        trail[n].append((axis, places[n], sizes[n], whole))

    def add(n, step):
        axis, was, size, whole = trail[n][step]
        me = here[axis[0]]
        buf = bufs[n][step]
        for copy in going[n]:
            copy.wait()
        if whole:
            piece = size
            value = buf[0]
        else:
            piece = size // axis[1]
            value = accs[n][pl.ds(me * piece, piece)]
            places[n] = was + me * piece
            sizes[n] = piece
        for k in range(1, axis[1]):
            value = value + buf[k]
        if step == 3:
            out[pl.ds(places[n], piece)] = value
        else:
            accs[n][pl.ds(0, piece)] = value

    def gather(n, step):
        axis, was, size, whole = trail[n][step]
        copies = []
        if not whole:
            some = out.at[pl.ds(places[n], sizes[n])]
            for d in range(1, axis[1]):
                copies.append(send(some, some, ss.at[n, 4 + step, d], rs.at[n, 4 + step, d], peer(axis, d)[1]))
        going[n] = copies
        started.extend(copies)

    def forward(n, d):
        axis = PARTS[n][2][1]
        some = out.at[pl.ds(trail[n][1][1] + peer(axis, axis[1] - d)[0] * sizes[n], sizes[n])]
        return send(some, some, ss.at[n, 4, d], rs.at[n, 4, d], peer(C, 1)[1])

    for step in (1, 2, 3):
        for n in range(number):
            add(n, step)
            if step < 3:
                scatter(n, step + 1)
            else:
                gather(n, 3)
    for step in (2, 1):
        for n in range(number):
            for copy in going[n]:
                copy.wait_recv()
            if not trail[n][step + 1][3]:
                places[n], sizes[n] = trail[n][step + 1][1:3]
            gather(n, step)
            if step == 1:
                going[n] = list(enumerate(going[n], 1)), [forward(n, 0)]
    for n in range(number):
        coming, passed = going[n]
        for d, copy in coming:
            copy.wait_recv()
            passed.append(forward(n, d))
        started += passed
    background()
    for n in range(number):
        for copy in going[n][1]:
            copy.wait_recv()
    for copy in started:
        copy.wait_send()


def first_part(rows, start, start_circ):
    bufs, accs = [], []
    for _, size, order in PARTS:
        for step, axis in enumerate(order):
            if size % axis[1] == 0:
                size = size // axis[1]
            bufs.append(VM((axis[1], size, 8, 128) if step else (size, 8, 128), F32))
            if step == 0:
                accs.append(VM((size, 8, 128), F32))
    dma = pltpu.SemaphoreType.DMA
    return pl.pallas_call(
        first_kernel,
        out_shape=(
            jax.ShapeDtypeStruct((128, 1024), F32),
            jax.ShapeDtypeStruct((64, 128), F32),
            jax.ShapeDtypeStruct((8, 6, 8, 1024), F32),
        ),
        in_specs=[pl.BlockSpec(memory_space=VM)] * 3,
        out_specs=(pl.BlockSpec(memory_space=VM),) * 3,
        scratch_shapes=[
            VM((8, 6, 16, 1024), F32),
            VM((8, 6, 16, 1024), F32),
            VM((16, 8, 128), F32),
            VM((16, 8, 128), F32),
            VM((16, 8, 128), F32),
            VM((16, 8, 128), F32),
            VM((6, 8, 8, 1024), F32),
            VM((1024, 384 * len(TERMS)), BF16),
            VM((384 * len(TERMS), 1024), BF16),
            VM((BLOCKS * 16, 8, 128), F32),
            VM((BLOCKS * 16, 8, 128), F32),
            VM((1024, 1024), BF16),
            VM((1024, 1024), BF16),
            VM((1024, 1024), BF16),
            dma((CHUNKS, 8)),
            dma((CHUNKS, 8)),
            dma((3, 16)),
            dma((3, 16)),
            dma((2, 8)),
            dma((2, 8)),
            dma((len(PARTS), 8, 8)),
            dma((len(PARTS), 8, 8)),
            *bufs,
            *accs,
        ],
        compiler_params=pltpu.CompilerParams(collective_id=0, has_side_effects=True, vmem_limit_bytes=LIMIT),
        name="first_part",
    )(rows, start, start_circ)


def core_kernel(basis, mine, early, factor, core, late):
    late[...] = early[...]
    last = basis[...].T
    factor[...] = last
    here = dot(mine[...].reshape(384, 1024), last)
    for k in range(48):
        core[pl.ds(k, 8, stride=48), :] = here[8 * k : 8 * k + 8]


def core_part(basis, mine, early):
    return pl.pallas_call(
        core_kernel,
        out_shape=(
            jax.ShapeDtypeStruct((1024, 128), F32),
            jax.ShapeDtypeStruct((384, 128), F32),
            jax.ShapeDtypeStruct((64, 128), F32),
        ),
        in_specs=[pl.BlockSpec(memory_space=VM)] * 3,
        out_specs=(pl.BlockSpec(memory_space=VM),) * 3,
        compiler_params=pltpu.CompilerParams(vmem_limit_bytes=LIMIT),
        name="core_part",
    )(basis, mine, early)


def local(record, start_time, start_circ):
    rows = record.reshape(96, 8, 8, 128).transpose(0, 2, 1, 3).reshape(6144, 128)
    basis, early, mine = first_part(rows, start_time.T, start_circ)
    factor_circ, core, late = core_part(basis, mine, early)
    return (late.T, factor_circ, core.reshape(8, 48, 128))


def solution(mesh):
    placed = (P("tm", "pts", None), P(), P())
    return jax.shard_map(
        local,
        mesh=mesh,
        in_specs=placed,
        out_specs=(P(), P(), P("tm", "pts", None)),
        check_vma=False,
    )
```
